256 devices in a mesh: seq: 16 (over z, core), kvh: 4 (over x), rep: 4 (over y).
Axes of the slice: x: 4, y: 4, z: 8, core: 2. Of those that a mesh axis runs over, the one named last changes fastest.
Arguments:
- prompt_kv: bfloat16 [64, 3072, 2048], P('rep', ('seq', 'kvh')), may hold values from -6 to 6
- prompt_len: int32 [64], replicated, may hold values from 1 to 3072, 122880 in all
- request_group: int32 [64], replicated, may hold values from 0 to 63, as said below
- res_kv: bfloat16 [262144, 2048], P(('seq', 'rep'), 'kvh'), may hold values from -6 to 6
- res_len: int32 [64, 31], P(('seq', 'rep')), may hold values from 1 to 2048, 4096 in all within a row
- queries: bfloat16 [2, 2048, 8192], P(None, ('seq', 'rep'), 'kvh'), may hold values from -6.5 to 6.5
- step_kv: bfloat16 [2, 2048, 2048], P(None, ('seq', 'rep'), 'kvh'), may hold values from -6.5 to 6.5
Outputs:
- attention: bfloat16 [2, 2048, 8192], P(None, ('seq', 'rep'), 'kvh')
- landed_cache: bfloat16 [196608, 2048], P(('seq', 'rep'), 'kvh')
The draws below stay inside these ranges and needn't reach their ends.
Inputs may be any that keep to these rules, and one draw needn't show every extreme that they name: `request_group`: request q lies in prefill group q // 16; its decode group is a seq index times 4 plus a rep index; every decode group receives exactly one request, and at most 4 requests of one prefill group go to one rep index.
All inputs are finite; a program needn't handle non-finite values.
Results may differ from the reference program's by a relative error of at most 0.0049.
Values may be sent and summed in bfloat16 or wider, within the bound.
A program may use at most 128 MiB of HBM per device.

```python
import math
import jax
import jax.numpy as jnp
import numpy as np
from jax import lax

HD = 128
KVH = 8
QH = 64
ROWS = 32
RES_TOK = 4096
STEPS = 2
GQA = 8
LEN_MAX = 3072
GROUPS = 64
PROMPT_TOTAL = 122880
RES_MOST = 2048
N_SEQ = 16
N_REP = 4


def draw_queries(key, part):
    key = jax.random.fold_in(key, 11)
    shape = (STEPS, GROUPS * ROWS, QH * HD)
    base = jnp.clip(jax.random.normal(key, shape, jnp.float32), -4.5, 4.5)
    return base.astype(jnp.bfloat16)


def draw_step_kv(key, part):
    key = jax.random.fold_in(key, 13)
    shape = (STEPS, GROUPS * ROWS, KVH * 2 * HD)
    base = jnp.clip(jax.random.normal(key, shape, jnp.float32), -4.5, 4.5)
    return base.astype(jnp.bfloat16)


def draw_request_group(key, part):
    key = jax.random.fold_in(key, 5)
    key_offset, key_order, key_seats = jax.random.split(key, 3)
    offset = jax.random.randint(key_offset, (), 0, N_REP)
    order = jax.vmap(lambda item: jax.random.permutation(item, N_SEQ))(jax.random.split(key_order, N_REP))
    prefill_ids = jnp.arange(N_REP, dtype=jnp.int32)[:, None]
    rep_dest = ((prefill_ids + order + offset) % N_REP).reshape(-1)
    req_ids = jnp.arange(N_SEQ * N_REP, dtype=jnp.int32)
    same_rep = rep_dest[None, :] == rep_dest[:, None]
    earlier = req_ids[None, :] < req_ids[:, None]
    rank_in = jnp.sum(same_rep & earlier, axis=1).astype(jnp.int32)
    seats = jax.vmap(lambda item: jax.random.permutation(item, N_SEQ))(jax.random.split(key_seats, N_REP))
    seq_dest = seats[rep_dest, rank_in]
    return (seq_dest * N_REP + rep_dest).astype(jnp.int32)


def shard_levels(own_key, shape, cuts, smallest, high):
    factor_of, own = 1.0, jax.random.fold_in(own_key, 6)
    for axis_at, parts in cuts:
        heights = jnp.exp(jax.random.uniform(jax.random.fold_in(own, axis_at), (parts,), jnp.float32, smallest / len(cuts), high / len(cuts)))
        factor_of = factor_of * jnp.repeat(heights, shape[axis_at] // parts).reshape([-1 if axis == axis_at else 1 for axis in range(len(shape))])
    return factor_of


def split_up(count, total, limit, lean):
    loads = [(1 << 20) // math.isqrt(rank ** lean) + 1 for rank in range(2, count + 1)]
    rest, given = total - limit - (count - 1), [1] * (count - 1)
    while rest > 0:
        candidates = [i for i in range(count - 1) if given[i] < limit]
        whole, left = sum([loads[i] for i in candidates]), rest
        for i in candidates:
            more = min(limit - given[i], max(1, left * loads[i] // whole), rest)
            given[i] = given[i] + more
            rest = rest - more
    return np.array([limit] + given)


def ragged(own_key, amount, total, limit, skew):
    if amount == 2:
        one = jax.random.randint(own_key, (), max(1, total - limit), min(limit, total - 1) + 1)
        return jnp.stack([one, total - one])
    sizes = jnp.asarray(split_up(amount, total, limit, skew), jnp.int32)
    twos = (amount - 1) // 2
    source_of, taker = sizes[1:1 + 2 * twos:2], sizes[2:2 + 2 * twos:2]
    margin = jnp.minimum(source_of - 1, limit - taker)
    passed = jax.random.randint(jax.random.fold_in(own_key, 1), (twos,), 0, 1 << 20) % (margin + 1)
    sizes = sizes.at[1:1 + 2 * twos:2].set(source_of - passed).at[2:2 + 2 * twos:2].set(taker + passed)
    return sizes[jax.random.permutation(jax.random.fold_in(own_key, 2), amount)]


def bell_draw(rng, dims, width, reach, shards=(), kind=jnp.bfloat16):
    loudness = shard_levels(rng, dims, shards, -0.22, 0.18) if shards else 1.0
    array = jax.random.normal(rng, dims, jnp.float32) * width * loudness
    return jnp.minimum(jnp.maximum(array, -reach), reach).astype(kind)


def setup_inputs(seed: int = 0) -> dict:
    keys = jax.random.split(jax.random.key(seed), 8)
    prompt_kv = bell_draw(keys[0], (GROUPS, LEN_MAX, KVH * 2 * HD), 1.0, 6.0, ((0, 4), (1, 64)))
    prompt_len = ragged(keys[1], GROUPS, PROMPT_TOTAL, LEN_MAX, 1).astype(jnp.int32)
    request_group = draw_request_group(jax.random.fold_in(keys[7], 71), 0)
    res_kv = bell_draw(keys[3], (GROUPS * RES_TOK, KVH * 2 * HD), 1.0, 6.0, ((0, 64), (1, 4)))
    res_len = jax.vmap(lambda own: ragged(own, ROWS - 1, RES_TOK, RES_MOST, 2))(jax.random.split(keys[4], GROUPS)).reshape((GROUPS, ROWS - 1)).astype(jnp.int32)
    queries = draw_queries(jax.random.fold_in(keys[7], 71), 0)
    step_kv = draw_step_kv(jax.random.fold_in(keys[7], 71), 0)
    return dict(prompt_kv=prompt_kv, prompt_len=prompt_len, request_group=request_group, res_kv=res_kv, res_len=res_len, queries=queries, step_kv=step_kv)


def attend_group(res_block, lengths, land_block, own_len, query_group, fresh_group):
    cache_rows = jnp.concatenate([res_block, land_block], axis=0).astype(jnp.float32)
    total_rows = cache_rows.shape[0]
    row_ends = jnp.cumsum(lengths)
    starts = row_ends - lengths
    res_pos = jnp.arange(RES_TOK, dtype=jnp.int32)
    member_res = (res_pos[None, :] >= starts[:, None]) & (res_pos[None, :] < row_ends[:, None])
    member_res = jnp.concatenate([member_res, jnp.zeros((1, RES_TOK), bool)], axis=0)
    land_pos = jnp.arange(LEN_MAX, dtype=jnp.int32)
    member_new = jnp.concatenate([jnp.zeros((ROWS - 1, LEN_MAX), bool), (land_pos < own_len)[None, :]], axis=0)
    member = jnp.concatenate([member_res, member_new], axis=1)
    split_rows = cache_rows.reshape(total_rows, KVH, 2, HD)
    head_keys = split_rows[:, :, 0]
    values = split_rows[:, :, 1]
    fresh_rows = fresh_group.astype(jnp.float32).reshape(STEPS, ROWS, KVH, 2, HD)
    score_scale = HD ** -0.5
    step_outputs = []
    for step in range(STEPS):
        query = query_group[step].astype(jnp.float32).reshape(ROWS, KVH, GQA, HD)
        scores = jnp.einsum('bjgd,cjd->bjgc', query, head_keys) * score_scale
        scores = jnp.where(member[:, None, None, :], scores, -1e30)
        fresh = jnp.einsum('bjgd,ubjd->bjgu', query, fresh_rows[:step + 1, :, :, 0]) * score_scale
        row_max = jnp.maximum(jnp.max(scores, axis=-1), jnp.max(fresh, axis=-1))
        weight_cache = jnp.exp(scores - row_max[..., None])
        weight_fresh = jnp.exp(fresh - row_max[..., None])
        row_total = jnp.sum(weight_cache, axis=-1) + jnp.sum(weight_fresh, axis=-1)
        rounded_cache = (weight_cache / row_total[..., None]).astype(jnp.bfloat16)
        rounded_fresh = (weight_fresh / row_total[..., None]).astype(jnp.bfloat16)
        rounded_cache = lax.optimization_barrier(rounded_cache).astype(jnp.float32)
        rounded_fresh = lax.optimization_barrier(rounded_fresh).astype(jnp.float32)
        mixed = jnp.einsum('bjgc,cjd->bjgd', rounded_cache, values)
        mixed = mixed + jnp.einsum('bjgu,ubjd->bjgd', rounded_fresh, fresh_rows[:step + 1, :, :, 1])
        step_outputs.append(mixed.reshape(ROWS, QH * HD).astype(jnp.bfloat16))
    return jnp.stack(step_outputs)


def reference(prompt_kv, prompt_len, request_group, res_kv, res_len, queries, step_kv):
    group_count = N_SEQ * N_REP
    req_ids = jnp.arange(group_count, dtype=jnp.int32)

    def land(group_id):
        is_mine = request_group == group_id
        source = jnp.sum(jnp.where(is_mine, req_ids, 0)).astype(jnp.int32)
        length = jnp.sum(jnp.where(is_mine, prompt_len, 0)).astype(jnp.int32)
        block = lax.dynamic_index_in_dim(prompt_kv, source, 0, keepdims=False)
        positions = jnp.arange(LEN_MAX, dtype=jnp.int32)
        block = jnp.where((positions < length)[:, None], block, jnp.zeros_like(block))
        return block, length

    landed, land_lengths = lax.map(land, jnp.arange(group_count, dtype=jnp.int32))
    res_blocks = res_kv.reshape(group_count, RES_TOK, KVH * 2 * HD)
    query_groups = queries.reshape(STEPS, group_count, ROWS, QH * HD).transpose(1, 0, 2, 3)
    fresh_groups = step_kv.reshape(STEPS, group_count, ROWS, KVH * 2 * HD).transpose(1, 0, 2, 3)

    def attend_one(pack):
        return attend_group(pack[0], pack[1], pack[2], pack[3], pack[4], pack[5])

    attention = lax.map(attend_one, (res_blocks, res_len, landed, land_lengths, query_groups, fresh_groups))
    attention = attention.transpose(1, 0, 2, 3).reshape(STEPS, group_count * ROWS, QH * HD)
    return attention, landed.reshape(group_count * LEN_MAX, KVH * 2 * HD)
```

```python
import functools
import jax
import jax.numpy as jnp
from jax import lax
from jax.experimental import pallas as pl
from jax.experimental.pallas import tpu as pltpu
from jax.sharding import PartitionSpec as P

HD = 128
STEPS = 2
CORES = 2
BLK = 16
NEG = -1e30
MESH = pl.DeviceIdType.MESH
EXP2_SCALE = (HD ** -0.5) * 1.4426950408889634
BF16 = jnp.bfloat16
F32 = jnp.float32
NT = (((1,), (1,)), ((), ()))


def wrap(value, size):
    return lax.rem(value + size, size)


def iota(shape, dim):
    return lax.broadcasted_iota(jnp.int32, shape, dim)


def kernel(cfg, prompt, plen_s, rgroup_s, plen_v, rgroup_v, res, rlen, queries, fresh, att_out, land_out, *scratch):
    n_seq, n_kvh, n_rep = cfg["mesh"]
    n_z = n_seq // CORES
    n_req, shard, _ = prompt.shape
    width = land_out.shape[3]
    blocks = shard // BLK
    per_rep = n_req // n_rep
    heads = width // (2 * HD)
    rows = queries.shape[1]
    gqa = queries.shape[2] // (heads * HD)
    q_rows = STEPS * gqa * rows
    res_tok = res.shape[0]
    chunks = cfg["chunks"]
    nc = len(chunks)
    it = iter(scratch)
    pv = [next(it) for _ in range(blocks)]
    s1 = [next(it) for _ in chunks]
    r1 = [next(it) for _ in chunks]
    s2 = [next(it) for _ in chunks]
    land, kcat, vcat, qcat, qv, fv, accs, sums, maxs, attv, tab_v, tab_s = (next(it) for _ in range(12))
    load_sem, send1, recv1, send2, recv2, out_sem = (next(it) for _ in range(6))

    seq, kvh, rep = lax.axis_index("seq"), lax.axis_index("kvh"), lax.axis_index("rep")
    zed, core = seq // CORES, lax.rem(seq, CORES)
    plane = [(a, b) for a in (2, 1, 3, 0) for b in (2, 1, 3, 0) if (a, b) != (0, 0)]
    line = [(a, b) for a in (4, 3, 5, 2, 6, 1, 7, 0) for b in (0, 1) if (a, b) != (0, 0)]

    def plane_peer(off):
        return lax.rem(kvh + off[0], n_kvh), lax.rem(rep + off[1], n_rep)

    def line_peer(off):
        return lax.rem(zed + off[0], n_z) * CORES + lax.rem(core + off[1], CORES)

    loads = [pltpu.make_async_copy(prompt.at[:, pl.ds(b * BLK, BLK), :], pv[b], load_sem.at[b]) for b in range(blocks)]
    for copy in loads:
        copy.start()
    others = []
    for h in range(heads):
        for at, dst in ((0, kcat), (HD, vcat)):
            others.append((res.at[:, pl.ds(2 * h * HD + at, HD)], dst.at[h, pl.ds(0, res_tok), pl.ds(0, HD)]))
    others += [(queries, qv), (fresh, fv)]
    others = [pltpu.make_async_copy(a, b, load_sem.at[blocks + i]) for i, (a, b) in enumerate(others)]
    for copy in others:
        copy.start()

    barrier = pltpu.get_barrier_semaphore()
    for off in plane:
        k2, r2 = plane_peer(off)
        pl.semaphore_signal(barrier, inc=1, device_id=(seq, k2, r2), device_id_type=MESH)
    for off in line:
        pl.semaphore_signal(barrier, inc=1, device_id=(line_peer(off), kvh, rep), device_id_type=MESH)

    packed, power = [0] * n_rep, [1] * n_rep
    for q in range(n_req):
        to_rep = lax.rem(rgroup_s[rep * n_req + q], n_rep)
        for d in range(n_rep):
            hit = to_rep == lax.rem(rep + d, n_rep)
            packed[d] = packed[d] + jnp.where(hit, power[d] * q, 0)
            power[d] = jnp.where(hit, power[d] * n_req, power[d])
    bits = n_req.bit_length() - 1

    def request_at(d, j):
        return (packed[d] >> (bits * j)) & (n_req - 1)

    def send_plane(c):
        b, c0, w = chunks[c]
        for i, off in enumerate(plane + [(0, 0)]):
            k2, r2 = plane_peer(off)
            cols = pl.ds(pl.multiple_of(k2 * width + c0, HD), w)
            for j in range(per_rep):
                piece = pv[b][request_at(off[1], j), :, cols]
                if off == (0, 0):
                    r1[c][(kvh * n_rep + rep) * per_rep + j] = piece
                else:
                    s1[c][i * per_rep + j] = piece
        if c == 0:
            pl.semaphore_wait(barrier, len(plane) + len(line))
        for i, off in enumerate(plane):
            k2, r2 = plane_peer(off)
            pltpu.make_async_remote_copy(
                src_ref=s1[c].at[pl.ds(i * per_rep, per_rep)],
                dst_ref=r1[c].at[pl.ds((kvh * n_rep + rep) * per_rep, per_rep)],
                send_sem=send1.at[c],
                recv_sem=recv1.at[c],
                device_id=(seq, k2, r2),
                device_id_type=MESH,
            ).start()

    landed_at = lambda c, s, n: land.at[pl.ds(s, n), :, pl.ds(chunks[c][0] * BLK, BLK), pl.ds(chunks[c][1], chunks[c][2])]

    def send_line(c):
        b, c0, w = chunks[c]
        for i, off in enumerate(line + [(0, 0)]):
            s_to = line_peer(off)
            slot, length = jnp.clip(tab_s[s_to, 0], 0, n_rep * per_rep - 1), tab_s[s_to, 1]
            for k in range(n_kvh):
                piece = r1[c][k * n_rep * per_rep + slot]
                at = (seq * n_kvh + k) * shard + b * BLK + iota((BLK, w), 0)
                piece = jnp.where(at < length, piece, jnp.zeros_like(piece))
                if off == (0, 0):
                    land[seq, k, pl.ds(b * BLK, BLK), pl.ds(c0, w)] = piece
                else:
                    s2[c][i, k] = piece
        for i, off in enumerate(line):
            pltpu.make_async_remote_copy(
                src_ref=s2[c].at[pl.ds(i, 1)],
                dst_ref=landed_at(c, seq, 1),
                send_sem=send2.at[c],
                recv_sem=recv2.at[c],
                device_id=(line_peer(off), kvh, rep),
                device_id_type=MESH,
            ).start()

    for c in range(nc):
        if c == 0 or chunks[c][0] != chunks[c - 1][0]:
            loads[chunks[c][0]].wait()
        send_plane(c)

    total_req = rgroup_v.shape[1]
    groups = rgroup_v[...]
    mine = (lax.rem(groups, n_rep) == rep).astype(BF16)
    earlier = (iota((total_req, total_req), 0) < iota((total_req, total_req), 1)).astype(BF16)
    slots = jnp.dot(jnp.broadcast_to(mine, (n_seq, total_req)), earlier, preferred_element_type=F32)
    goes = jnp.broadcast_to(groups, (n_seq, total_req)) == iota((n_seq, total_req), 0) * n_rep + rep
    slot_of = jnp.sum(jnp.where(goes, slots, 0.0), axis=1, keepdims=True)
    len_of = jnp.sum(jnp.where(goes, plen_v[...].astype(F32), 0.0), axis=1, keepdims=True)
    lane = iota((n_seq, HD), 1)
    tab_v[...] = jnp.where(lane == 0, slot_of, len_of).astype(jnp.int32)
    to_smem = pltpu.make_async_copy(tab_v, tab_s, load_sem.at[blocks + len(others)])
    to_smem.start()
    to_smem.wait()

    for c in range(nc):
        pltpu.make_async_copy(
            r1[c].at[pl.ds(0, len(plane) * per_rep)], r1[c].at[pl.ds(0, len(plane) * per_rep)], recv1.at[c]
        ).wait()
        send_line(c)

    for copy in others:
        copy.wait()
    n_keys = kcat.shape[1]
    lens = rlen[...].astype(F32)
    diagonal = jnp.where(iota((rows, rows - 1), 0) == iota((rows, rows - 1), 1), lens, 0.0)
    column = jnp.sum(diagonal, axis=1, keepdims=True)
    above = iota((rows, HD), 0) - iota((rows, HD), 1)
    ends = jnp.sum(jnp.where(above <= 0, column, 0.0), axis=0, keepdims=True).astype(jnp.int32)
    starts = jnp.sum(jnp.where(above < 0, column, 0.0), axis=0, keepdims=True).astype(jnp.int32)

    def hide(i, carry):
        key = i * 256 + iota((256, HD), 0)
        hidden = ((key < starts) | (key >= ends)) & (iota((256, HD), 1) < rows)
        hidden = hidden.astype(F32).astype(BF16)
        at = pl.ds(pl.multiple_of(i * 256, 256), 256)
        for h in range(heads):
            kcat[h, at, pl.ds(HD, HD)] = hidden
            vcat[h, at, pl.ds(HD, HD)] = jnp.ones((256, HD), BF16)
        return carry

    lax.fori_loop(0, res_tok // 256, hide, 0)
    rest = n_keys - res_tok
    key, lane = iota((rest, HD), 0), iota((rest, HD), 1)
    hidden = ((lane < rows) & (lane != lax.rem(key, rows))) | ((lane == rows) & (key >= rows)) | (
        (lane == rows + 1) & (key >= STEPS * rows)
    )
    hidden = hidden.astype(F32).astype(BF16)
    pad = jnp.zeros((rest - STEPS * rows, HD), BF16)
    for h in range(heads):
        kcat[h, pl.ds(res_tok, rest), pl.ds(HD, HD)] = hidden
        vcat[h, pl.ds(res_tok, rest), pl.ds(HD, HD)] = jnp.ones((rest, HD), BF16)
        for at, dst in ((0, kcat), (HD, vcat)):
            for u in range(STEPS):
                dst[h, pl.ds(res_tok + u * rows, rows), pl.ds(0, HD)] = fv[u, :, pl.ds(2 * h * HD + at, HD)]
            dst[h, pl.ds(res_tok + STEPS * rows, rest - STEPS * rows), pl.ds(0, HD)] = pad
    row, lane = iota((rows, HD), 0), iota((rows, HD), 1)
    for t in range(STEPS):
        aside = (lane == row) | (lane == rows + 1)
        if t == 0:
            aside = aside | (lane == rows)
        aside = jnp.where(aside, NEG, 0.0).astype(BF16)
        for h in range(heads):
            for g in range(gqa):
                at = pl.ds((t * gqa + g) * rows, rows)
                qcat[h, at, pl.ds(0, HD)] = qv[t, :, pl.ds((h * gqa + g) * HD, HD)]
                qcat[h, at, pl.ds(HD, HD)] = aside

    q_tile = cfg["q_tile"]
    tiles = q_rows // q_tile

    def attend(i, carry):
        h, at = i // tiles, pl.ds(pl.multiple_of(lax.rem(i, tiles) * q_tile, q_tile), q_tile)
        scores = lax.dot_general(qcat[h, at, :], kcat[h], NT, preferred_element_type=F32)
        top = jnp.max(scores, axis=1, keepdims=True)
        weights = jnp.exp2((scores - top) * EXP2_SCALE).astype(BF16)
        mixed = jnp.dot(weights, vcat[h], preferred_element_type=F32)
        accs[h, at, :] = mixed[:, :HD]
        sums[h, at, :] = mixed[:, HD:]
        maxs[h, at, :] = jnp.broadcast_to(top, (q_tile, HD))
        return carry

    lax.fori_loop(0, heads * tiles, attend, 0)

    few = STEPS * gqa
    pick = (iota((few, q_rows), 1) == iota((few, q_rows), 0) * rows + (rows - 1)).astype(F32).astype(BF16)
    last = pl.ds(rows - 1, few, stride=rows)
    own_len = tab_s[seq, 1]
    asks, parts = [], []
    for h in range(heads):
        asks.append(jnp.dot(pick, qcat[h, :, pl.ds(0, HD)], preferred_element_type=F32).astype(BF16))
        parts.append([(maxs[h, last, :], sums[h, last, :], accs[h, last, :])])
    for h in range(heads):
        accs[h] = accs[h] / sums[h]

    keys_blk = n_seq * n_kvh * BLK
    n_at = iota((few, keys_blk), 1)
    n_at = (n_at // BLK) * shard + lax.rem(n_at, BLK)
    outs = []
    arrived = set()
    for c, (b, c0, w) in enumerate(chunks):
        pltpu.make_async_copy(landed_at(c, 0, len(line)), landed_at(c, 0, len(line)), recv2.at[c]).wait()
        out = pltpu.make_async_copy(
            landed_at(c, 0, n_seq),
            land_out.at[:, :, pl.ds(b * BLK, BLK), pl.ds(c0, w)],
            out_sem.at[c],
        )
        out.start()
        outs.append(out)
        arrived |= {(b, at) for at in range(c0, c0 + w, HD)}
        for h in range(heads):
            k_at, v_at = 2 * h * HD, (2 * h + 1) * HD
            if not {(b, k_at), (b, v_at)} <= arrived:
                continue
            arrived -= {(b, k_at), (b, v_at)}
            keys = land[:, :, pl.ds(b * BLK, BLK), pl.ds(k_at, HD)].reshape(keys_blk, HD)
            values = land[:, :, pl.ds(b * BLK, BLK), pl.ds(v_at, HD)].reshape(keys_blk, HD)
            scores = lax.dot_general(asks[h], keys, NT, preferred_element_type=F32)
            scores = jnp.where(n_at + b * BLK < own_len, scores, NEG)
            top = jnp.max(scores, axis=1, keepdims=True)
            weights = jnp.exp2((scores - top) * EXP2_SCALE)
            total = jnp.sum(weights, axis=1, keepdims=True)
            mixed = jnp.dot(weights.astype(BF16), values, preferred_element_type=F32)
            parts[h].append((top, total, mixed))
    for h in range(heads):
        top = functools.reduce(jnp.maximum, [m for m, _, _ in parts[h]])
        total, mixed = 0.0, 0.0
        for m, l, a in parts[h]:
            factor = jnp.exp2((m - top) * EXP2_SCALE)
            total, mixed = total + factor * l, mixed + factor * a
        accs[h, last, :] = mixed / total
        for t in range(STEPS):
            for g in range(gqa):
                attv[t, :, pl.ds((h * gqa + g) * HD, HD)] = accs[h, pl.ds((t * gqa + g) * rows, rows), :].astype(BF16)
    out = pltpu.make_async_copy(attv, att_out, out_sem.at[nc])
    out.start()
    outs.append(out)
    for c in range(nc):
        pltpu.make_async_copy(s1[c], s1[c], send1.at[c]).wait()
        pltpu.make_async_copy(s2[c], s2[c], send2.at[c]).wait()
    for out in outs:
        out.wait()


def per_device(mesh_shape, prompt_kv, prompt_len, request_group, res_kv, res_len, queries, step_kv):
    n_seq, n_kvh, n_rep = mesh_shape
    n_req, shard, all_cols = prompt_kv.shape
    width = all_cols // n_kvh
    per_rep = n_req // n_rep
    heads = width // (2 * HD)
    blocks = shard // BLK
    rows, q_cols = queries.shape[1:]
    q_rows = STEPS * rows * (q_cols // (heads * HD))
    chunks = [(b, c0, 2 * HD) for b in range(blocks) for c0 in range(0, width, 2 * HD)]
    n_keys = res_kv.shape[0] + 256
    cfg = dict(mesh=mesh_shape, chunks=chunks, q_tile=128)
    near, far = n_kvh * n_rep, n_seq
    v = lambda shape, dtype=BF16: pltpu.VMEM(shape, dtype)
    dma = lambda n: pltpu.SemaphoreType.DMA((n,))
    scratch = (
        [v((n_req, BLK, all_cols)) for _ in range(blocks)]
        + [v(((near - 1) * per_rep, BLK, w)) for _, _, w in chunks]
        + [v((near * per_rep, BLK, w)) for _, _, w in chunks]
        + [v((far - 1, n_kvh, BLK, w)) for _, _, w in chunks]
        + [
            v((n_seq, n_kvh, shard, width)),
            v((heads, n_keys, 2 * HD)),
            v((heads, n_keys, 2 * HD)),
            v((heads, q_rows, 2 * HD)),
            v(queries.shape),
            v(step_kv.shape),
            v((heads, q_rows, HD), F32),
            v((heads, q_rows, HD), F32),
            v((heads, q_rows, HD), F32),
            v(queries.shape),
            v((n_seq, HD), jnp.int32),
            pltpu.SMEM((n_seq, HD), jnp.int32),
        ]
        + [dma(blocks + 2 * heads + 3)]
        + [dma(len(chunks))] * 4
        + [dma(len(chunks) + 1)]
    )
    spec = lambda space: pl.BlockSpec(memory_space=space)
    attention, landed = pl.pallas_call(
        functools.partial(kernel, cfg),
        out_shape=(
            jax.ShapeDtypeStruct(queries.shape, BF16),
            jax.ShapeDtypeStruct((n_seq, n_kvh, shard, width), BF16),
        ),
        in_specs=[spec(s) for s in (pl.ANY, pltpu.SMEM, pltpu.SMEM, pltpu.VMEM, pltpu.VMEM, pl.ANY, pltpu.VMEM, pl.ANY, pl.ANY)],
        out_specs=(spec(pl.ANY), spec(pl.ANY)),
        scratch_shapes=scratch,
        compiler_params=pltpu.CompilerParams(collective_id=0, has_side_effects=True, vmem_limit_bytes=56 << 20),
    )(
        prompt_kv,
        prompt_len,
        request_group,
        prompt_len.reshape(1, -1),
        request_group.reshape(1, -1),
        res_kv,
        res_len,
        queries,
        step_kv,
    )
    return attention, landed.reshape(n_seq * n_kvh * shard, width)


def solution(mesh):
    in_specs = (
        P("rep", ("seq", "kvh"), None),
        P(),
        P(),
        P(("seq", "rep"), "kvh"),
        P(("seq", "rep"), None),
        P(None, ("seq", "rep"), "kvh"),
        P(None, ("seq", "rep"), "kvh"),
    )
    out_specs = (P(None, ("seq", "rep"), "kvh"), P(("seq", "rep"), "kvh"))
    shape = tuple(mesh.shape[a] for a in ("seq", "kvh", "rep"))
    return jax.shard_map(
        functools.partial(per_device, shape), mesh=mesh, in_specs=in_specs, out_specs=out_specs, check_vma=False
    )
```

```python
import functools
import jax
import jax.numpy as jnp
from jax import lax
from jax.experimental import pallas as pl
from jax.experimental.pallas import tpu as pltpu
from jax.sharding import PartitionSpec as P

HD = 128
STEPS = 2
CORES = 2
BLK = 16
NEG = -1e30
MESH = pl.DeviceIdType.MESH
EXP2_SCALE = (HD ** -0.5) * 1.4426950408889634
BF16 = jnp.bfloat16
F32 = jnp.float32
NT = (((1,), (1,)), ((), ()))
AHEAD = 4
ALL = (0, 1, 2, 3)
CHUNKS = [
    (0, 0, 128, (0,)),
    (0, 0, 128, (1,)),
    (0, 0, 128, (2, 3)),
    (0, 128, 128, ALL),
    (0, 256, 256, ALL),
    (1, 0, 512, ALL),
    (2, 0, 512, ALL),
]


def wrap(value, size):
    return lax.rem(value + size, size)


def iota(shape, dim):
    return lax.broadcasted_iota(jnp.int32, shape, dim)


def kernel(cfg, prompt, plen_s, rgroup_s, plen_v, rgroup_v, res, rlen, queries, fresh, attv, land, *scratch):
    n_seq, n_kvh, n_rep = cfg["mesh"]
    n_z = n_seq // CORES
    n_req, shard, _ = prompt.shape
    width = land.shape[3]
    blocks = shard // BLK
    per_rep = n_req // n_rep
    heads = width // (2 * HD)
    rows = queries.shape[1]
    gqa = queries.shape[2] // (heads * HD)
    q_rows = STEPS * gqa * rows
    res_tok = res.shape[0]
    chunks = cfg["chunks"]
    nc = len(chunks)
    it = iter(scratch)
    pieces = sorted({chunk[:3] for chunk in chunks})
    pv = [next(it) for _ in pieces]
    s1 = [next(it) for _ in chunks]
    r1 = [next(it) for _ in chunks]
    s2 = [next(it) for _ in chunks]
    kcat, vcat, qcat, qv, fv, accs, sums, maxs, tab_v, tab_s = (next(it) for _ in range(10))
    load_sem, send1, recv1, send2, recv2 = (next(it) for _ in range(5))

    seq, kvh, rep = lax.axis_index("seq"), lax.axis_index("kvh"), lax.axis_index("rep")
    zed, core = seq // CORES, lax.rem(seq, CORES)
    plane = [(a, b) for a in (2, 3, 1, 0) for b in (2, 1, 3, 0) if (a, b) != (0, 0)]
    line = [(a, b) for a in (4, 3, 5, 2, 6, 1, 7, 0) for b in (0, 1) if (a, b) != (0, 0)]

    kvh_peer = [kvh, kvh + 1 - 2 * lax.rem(kvh, 2), lax.rem(kvh + 2, 4), 3 - kvh]

    def plane_peer(off):
        return kvh_peer[off[0]], lax.rem(rep + off[1], n_rep)

    def first_slab(c):
        steps = chunks[c][3]
        return 0 if steps == ALL else 2 - 2 * (kvh // 2) if steps == (2, 3) else kvh_peer[steps[0]]

    def own_place(c):
        steps = chunks[c][3]
        return kvh if steps == ALL else lax.rem(kvh, 2) if steps == (2, 3) else 0

    def line_peer(off):
        return lax.rem(zed + off[0], n_z) * CORES + lax.rem(core + off[1], CORES)

    def loads(p):
        b, c0, w = pieces[p]
        return [
            pltpu.make_async_copy(
                prompt.at[:, pl.ds(b * BLK, BLK), pl.ds(k * width + c0, w)], pv[p].at[k], load_sem.at[p * n_kvh + k]
            )
            for k in range(n_kvh)
        ]

    for copy in loads(0):
        copy.start()
    others = []
    for h in range(heads):
        for at, dst in ((0, kcat), (HD, vcat)):
            others.append((res.at[:, pl.ds(2 * h * HD + at, HD)], dst.at[h, pl.ds(0, res_tok), pl.ds(0, HD)]))
    others += [(queries, qv), (fresh, fv)]
    others = [pltpu.make_async_copy(a, b, load_sem.at[len(pieces) * n_kvh + i]) for i, (a, b) in enumerate(others)]

    barrier = pltpu.get_barrier_semaphore()
    for off in plane:
        k2, r2 = plane_peer(off)
        pl.semaphore_signal(barrier, inc=1, device_id=(seq, k2, r2), device_id_type=MESH)
    for off in line:
        pl.semaphore_signal(barrier, inc=1, device_id=(line_peer(off), kvh, rep), device_id_type=MESH)

    packed, power = [0] * n_rep, [1] * n_rep
    for q in range(n_req):
        to_rep = lax.rem(rgroup_s[rep * n_req + q], n_rep)
        for d in range(n_rep):
            hit = to_rep == lax.rem(rep + d, n_rep)
            packed[d] = packed[d] + jnp.where(hit, power[d] * q, 0)
            power[d] = jnp.where(hit, power[d] * n_req, power[d])
    bits = n_req.bit_length() - 1

    def request_at(d, j):
        return (packed[d] >> (bits * j)) & (n_req - 1)

    def send_plane(c):
        source, offs = pv[pieces.index(chunks[c][:3])], [off for off in plane if off[0] in chunks[c][3]]
        place = pl.ds((own_place(c) * n_rep + rep) * per_rep, per_rep)
        for i, off in enumerate(offs):
            k2, r2 = plane_peer(off)
            for j in range(per_rep):
                s1[c][i * per_rep + j] = source[k2, request_at(off[1], j)]
        if 0 in chunks[c][3]:
            for j in range(per_rep):
                r1[c][(own_place(c) * n_rep + rep) * per_rep + j] = source[kvh, request_at(0, j)]
        if c == 0:
            pl.semaphore_wait(barrier, len(plane) + len(line))
        for i, off in enumerate(offs):
            k2, r2 = plane_peer(off)
            pltpu.make_async_remote_copy(
                src_ref=s1[c].at[pl.ds(i * per_rep, per_rep)],
                dst_ref=r1[c].at[place],
                send_sem=send1.at[c],
                recv_sem=recv1.at[c],
                device_id=(seq, k2, r2),
                device_id_type=MESH,
            ).start()

    def landed_at(c, s, n, k):
        b, c0, w, steps = chunks[c]
        return land.at[pl.ds(s, n), pl.ds(k, len(steps)), pl.ds(b * BLK, BLK), pl.ds(c0, w)]

    def send_line(c):
        b, c0, w, steps = chunks[c]
        first = first_slab(c)
        for i, off in enumerate(line + [(0, 0)]):
            s_to = line_peer(off)
            slot, length = jnp.clip(tab_s[s_to, 0], 0, n_rep * per_rep - 1), tab_s[s_to, 1]
            for k in range(len(steps)):
                piece = r1[c][k * n_rep * per_rep + slot]
                at = (seq * n_kvh + first + k) * shard + b * BLK + iota((BLK, w), 0)
                piece = jnp.where(at < length, piece, jnp.zeros_like(piece))
                if off == (0, 0):
                    land[seq, first + k, pl.ds(b * BLK, BLK), pl.ds(c0, w)] = piece
                else:
                    s2[c][i, k] = piece
        for i, off in enumerate(line):
            pltpu.make_async_remote_copy(
                src_ref=s2[c].at[pl.ds(i, 1)],
                dst_ref=landed_at(c, seq, 1, first),
                send_sem=send2.at[c],
                recv_sem=recv2.at[c],
                device_id=(line_peer(off), kvh, rep),
                device_id_type=MESH,
            ).start()

    loaded = set()

    def feed(c):
        if c < nc:
            p = pieces.index(chunks[c][:3])
            if p not in loaded:
                loaded.add(p)
                for copy in loads(p):
                    copy.wait()
            send_plane(c)

    total_req = rgroup_v.shape[1]
    groups = rgroup_v[...]
    mine = (lax.rem(groups, n_rep) == rep).astype(BF16)
    earlier = (iota((total_req, total_req), 0) < iota((total_req, total_req), 1)).astype(BF16)
    slots = jnp.dot(jnp.broadcast_to(mine, (n_seq, total_req)), earlier, preferred_element_type=F32)
    goes = jnp.broadcast_to(groups, (n_seq, total_req)) == iota((n_seq, total_req), 0) * n_rep + rep
    slot_of = jnp.sum(jnp.where(goes, slots, 0.0), axis=1, keepdims=True)
    len_of = jnp.sum(jnp.where(goes, plen_v[...].astype(F32), 0.0), axis=1, keepdims=True)
    lane = iota((n_seq, HD), 1)
    tab_v[...] = jnp.where(lane == 0, slot_of, len_of).astype(jnp.int32)
    to_smem = pltpu.make_async_copy(tab_v, tab_s, load_sem.at[len(pieces) * n_kvh + len(others)])
    to_smem.start()
    feed(0)
    for p in range(1, len(pieces)):
        for copy in loads(p):
            copy.start()
    for copy in others:
        copy.start()
    for c in range(1, cfg["ahead"]):
        feed(c)
    to_smem.wait()

    for c in range(nc):
        came = r1[c].at[pl.ds(0, s1[c].shape[0])]
        pltpu.make_async_copy(came, came, recv1.at[c]).wait()
        send_line(c)
        feed(c + cfg["ahead"])

    for copy in others:
        copy.wait()
    n_keys = kcat.shape[1]
    lens = rlen[...].astype(F32)
    diagonal = jnp.where(iota((rows, rows - 1), 0) == iota((rows, rows - 1), 1), lens, 0.0)
    column = jnp.sum(diagonal, axis=1, keepdims=True)
    above = iota((rows, HD), 0) - iota((rows, HD), 1)
    ends = jnp.sum(jnp.where(above <= 0, column, 0.0), axis=0, keepdims=True).astype(jnp.int32)
    starts = jnp.sum(jnp.where(above < 0, column, 0.0), axis=0, keepdims=True).astype(jnp.int32)

    def hide(i, carry):
        key = i * 256 + iota((256, HD), 0)
        hidden = ((key < starts) | (key >= ends)) & (iota((256, HD), 1) < rows)
        hidden = hidden.astype(F32).astype(BF16)
        at = pl.ds(pl.multiple_of(i * 256, 256), 256)
        for h in range(heads):
            kcat[h, at, pl.ds(HD, HD)] = hidden
            vcat[h, at, pl.ds(HD, HD)] = jnp.ones((256, HD), BF16)
        return carry

    lax.fori_loop(0, res_tok // 256, hide, 0)
    rest = n_keys - res_tok
    key, lane = iota((rest, HD), 0), iota((rest, HD), 1)
    hidden = ((lane < rows) & (lane != lax.rem(key, rows))) | ((lane == rows) & (key >= rows)) | (
        (lane == rows + 1) & (key >= STEPS * rows)
    )
    hidden = hidden.astype(F32).astype(BF16)
    pad = jnp.zeros((rest - STEPS * rows, HD), BF16)
    for h in range(heads):
        kcat[h, pl.ds(res_tok, rest), pl.ds(HD, HD)] = hidden
        vcat[h, pl.ds(res_tok, rest), pl.ds(HD, HD)] = jnp.ones((rest, HD), BF16)
        for at, dst in ((0, kcat), (HD, vcat)):
            for u in range(STEPS):
                dst[h, pl.ds(res_tok + u * rows, rows), pl.ds(0, HD)] = fv[u, :, pl.ds(2 * h * HD + at, HD)]
            dst[h, pl.ds(res_tok + STEPS * rows, rest - STEPS * rows), pl.ds(0, HD)] = pad
    row, lane = iota((rows, HD), 0), iota((rows, HD), 1)
    for t in range(STEPS):
        aside = (lane == row) | (lane == rows + 1)
        if t == 0:
            aside = aside | (lane == rows)
        aside = jnp.where(aside, NEG, 0.0).astype(BF16)
        for h in range(heads):
            for g in range(gqa):
                at = pl.ds((t * gqa + g) * rows, rows)
                qcat[h, at, pl.ds(0, HD)] = qv[t, :, pl.ds((h * gqa + g) * HD, HD)]
                qcat[h, at, pl.ds(HD, HD)] = aside

    q_tile = cfg["q_tile"]
    tiles = q_rows // q_tile

    def attend(i, carry):
        h, at = i // tiles, pl.ds(pl.multiple_of(lax.rem(i, tiles) * q_tile, q_tile), q_tile)
        scores = lax.dot_general(qcat[h, at, :], kcat[h], NT, preferred_element_type=F32)
        top = jnp.max(scores, axis=1, keepdims=True)
        weights = jnp.exp2((scores - top) * EXP2_SCALE).astype(BF16)
        mixed = jnp.dot(weights, vcat[h], preferred_element_type=F32)
        accs[h, at, :] = mixed[:, :HD]
        sums[h, at, :] = mixed[:, HD:]
        maxs[h, at, :] = jnp.broadcast_to(top, (q_tile, HD))
        return carry

    lax.fori_loop(0, heads * tiles, attend, 0)

    few = STEPS * gqa
    pick = (iota((few, q_rows), 1) == iota((few, q_rows), 0) * rows + (rows - 1)).astype(F32).astype(BF16)
    last = pl.ds(rows - 1, few, stride=rows)
    own_len = tab_s[seq, 1]
    asks, parts = [], []
    for h in range(heads):
        asks.append(jnp.dot(pick, qcat[h, :, pl.ds(0, HD)], preferred_element_type=F32).astype(BF16))
        parts.append([(maxs[h, last, :], sums[h, last, :], accs[h, last, :])])
    for h in range(heads):
        accs[h] = accs[h] / sums[h]

    keys_blk = n_seq * n_kvh * BLK
    n_at = iota((few, keys_blk), 1)
    n_at = (n_at // BLK) * shard + lax.rem(n_at, BLK)
    arrived = set()
    for c, (b, c0, w, steps) in enumerate(chunks):
        came = landed_at(c, 0, len(line), 0)
        pltpu.make_async_copy(came, came, recv2.at[c]).wait()
        if steps in (ALL, (2, 3)):
            arrived |= {(b, at) for at in range(c0, c0 + w, HD)}
        for h in range(heads):
            k_at, v_at = 2 * h * HD, (2 * h + 1) * HD
            if not {(b, k_at), (b, v_at)} <= arrived:
                continue
            arrived -= {(b, k_at), (b, v_at)}
            keys = land[:, :, pl.ds(b * BLK, BLK), pl.ds(k_at, HD)].reshape(keys_blk, HD)
            values = land[:, :, pl.ds(b * BLK, BLK), pl.ds(v_at, HD)].reshape(keys_blk, HD)
            scores = lax.dot_general(asks[h], keys, NT, preferred_element_type=F32)
            scores = jnp.where(n_at + b * BLK < own_len, scores, NEG)
            top = jnp.max(scores, axis=1, keepdims=True)
            weights = jnp.exp2((scores - top) * EXP2_SCALE)
            total = jnp.sum(weights, axis=1, keepdims=True)
            mixed = jnp.dot(weights.astype(BF16), values, preferred_element_type=F32)
            parts[h].append((top, total, mixed))
    for h in range(heads):
        top = functools.reduce(jnp.maximum, [m for m, _, _ in parts[h]])
        total, mixed = 0.0, 0.0
        for m, l, a in parts[h]:
            factor = jnp.exp2((m - top) * EXP2_SCALE)
            total, mixed = total + factor * l, mixed + factor * a
        accs[h, last, :] = mixed / total
        for t in range(STEPS):
            for g in range(gqa):
                attv[t, :, pl.ds((h * gqa + g) * HD, HD)] = accs[h, pl.ds((t * gqa + g) * rows, rows), :].astype(BF16)
    for c in range(nc):
        pltpu.make_async_copy(s1[c], s1[c], send1.at[c]).wait()
        pltpu.make_async_copy(s2[c], s2[c], send2.at[c]).wait()


def store(attv, land, att_out, land_out, sem):
    copies = [pltpu.make_async_copy(attv, att_out, sem.at[0])]
    parts = land.shape[0] // 4
    for i in range(parts):
        copies.append(pltpu.make_async_copy(land.at[pl.ds(i * 4, 4)], land_out.at[pl.ds(i * 4, 4)], sem.at[1 + i]))
    for copy in copies:
        copy.start()
    for copy in copies:
        copy.wait()


def per_device(mesh_shape, prompt_kv, prompt_len, request_group, res_kv, res_len, queries, step_kv):
    n_seq, n_kvh, n_rep = mesh_shape
    n_req, shard, all_cols = prompt_kv.shape
    width = all_cols // n_kvh
    per_rep = n_req // n_rep
    heads = width // (2 * HD)
    blocks = shard // BLK
    rows, q_cols = queries.shape[1:]
    q_rows = STEPS * rows * (q_cols // (heads * HD))
    chunks = CHUNKS
    n_keys = res_kv.shape[0] + 256
    cfg = dict(mesh=mesh_shape, chunks=chunks, q_tile=128, ahead=AHEAD)
    pieces = sorted({chunk[:3] for chunk in chunks})
    v = lambda shape, dtype=BF16: pltpu.VMEM(shape, dtype)
    dma = lambda n: pltpu.SemaphoreType.DMA((n,))
    scratch = (
        [v((n_kvh, n_req, BLK, w)) for _, _, w in pieces]
        + [v(((len(d) * n_rep - (0 in d)) * per_rep, BLK, w)) for _, _, w, d in chunks]
        + [v((len(d) * n_rep * per_rep, BLK, w)) for _, _, w, d in chunks]
        + [v((n_seq - 1, len(d), BLK, w)) for _, _, w, d in chunks]
        + [
            v((heads, n_keys, 2 * HD)),
            v((heads, n_keys, 2 * HD)),
            v((heads, q_rows, 2 * HD)),
            v(queries.shape),
            v(step_kv.shape),
            v((heads, q_rows, HD), F32),
            v((heads, q_rows, HD), F32),
            v((heads, q_rows, HD), F32),
            v((n_seq, HD), jnp.int32),
            pltpu.SMEM((n_seq, HD), jnp.int32),
        ]
        + [dma(len(pieces) * n_kvh + 2 * heads + 3)]
        + [dma(len(chunks))] * 4
    )
    spec = lambda space: pl.BlockSpec(memory_space=space)
    held = pl.pallas_call(
        functools.partial(kernel, cfg),
        out_shape=(
            pltpu.VMEM(queries.shape, BF16),
            pltpu.VMEM((n_seq, n_kvh, shard, width), BF16),
        ),
        in_specs=[spec(s) for s in (pl.ANY, pltpu.SMEM, pltpu.SMEM, pltpu.VMEM, pltpu.VMEM, pl.ANY, pltpu.VMEM, pl.ANY, pl.ANY)],
        out_specs=(spec(pltpu.VMEM), spec(pltpu.VMEM)),
        scratch_shapes=scratch,
        compiler_params=pltpu.CompilerParams(collective_id=0, has_side_effects=True, vmem_limit_bytes=58 << 20),
    )(
        prompt_kv,
        prompt_len,
        request_group,
        prompt_len.reshape(1, -1),
        request_group.reshape(1, -1),
        res_kv,
        res_len,
        queries,
        step_kv,
    )
    attention, landed = pl.pallas_call(
        store,
        out_shape=tuple(jax.ShapeDtypeStruct(a.shape, a.dtype) for a in held),
        in_specs=[spec(pltpu.VMEM)] * 2,
        out_specs=(spec(pl.ANY), spec(pl.ANY)),
        scratch_shapes=[dma(1 + n_seq // 4)],
        compiler_params=pltpu.CompilerParams(vmem_limit_bytes=2 << 20),
    )(*held)
    return attention, landed.reshape(n_seq * n_kvh * shard, width)


def solution(mesh):
    in_specs = (
        P("rep", ("seq", "kvh"), None),
        P(),
        P(),
        P(("seq", "rep"), "kvh"),
        P(("seq", "rep"), None),
        P(None, ("seq", "rep"), "kvh"),
        P(None, ("seq", "rep"), "kvh"),
    )
    out_specs = (P(None, ("seq", "rep"), "kvh"), P(("seq", "rep"), "kvh"))
    shape = tuple(mesh.shape[a] for a in ("seq", "kvh", "rep"))
    return jax.shard_map(
        functools.partial(per_device, shape), mesh=mesh, in_specs=in_specs, out_specs=out_specs, check_vma=False
    )
```

```python
import functools
import jax
import jax.numpy as jnp
from jax import lax
from jax.experimental import pallas as pl
from jax.experimental.pallas import tpu as pltpu
from jax.sharding import PartitionSpec as P

HD = 128
STEPS = 2
CORES = 2
BLK = 16
NEG = -1e30
MESH = pl.DeviceIdType.MESH
EXP2_SCALE = (HD ** -0.5) * 1.4426950408889634
BF16 = jnp.bfloat16
F32 = jnp.float32
NT = (((1,), (1,)), ((), ()))
AHEAD = 4
LAST = 2
LATE_ORDER = [0, 1, 2, 3, 4, 5, 6, 7]
ALL = (0, 1, 2, 3)
CHUNKS = [
    (0, 0, 128, (0,)),
    (0, 0, 128, (1,)),
    (0, 0, 128, (2, 3)),
    (0, 128, 128, ALL),
    (0, 256, 256, ALL),
    (1, 0, 512, ALL),
    (2, 0, 256, ALL),
    (2, 256, 256, ALL),
]


def packed(values):
    return sum(v << (3 * i) for i, v in enumerate(values))


def nth_plane(p, zed):
    own = (packed([LATE_ORDER.index(i) for i in range(8)]) >> (3 * zed)) & 7
    at = p + (p >= own).astype(jnp.int32)
    return (packed(LATE_ORDER) >> (3 * at)) & 7


def wrap(value, size):
    return lax.rem(value + size, size)


def iota(shape, dim):
    return lax.broadcasted_iota(jnp.int32, shape, dim)


def kernel(cfg, prompt, groups_flat, plen, groups_row, res, res_len, queries, fresh, attv, land, *scratch):
    n_seq, n_kvh, n_rep = cfg["mesh"]
    n_z = n_seq // CORES
    n_req, shard, _ = prompt.shape
    width = land.shape[3]
    blocks = shard // BLK
    per_rep = n_req // n_rep
    heads = width // (2 * HD)
    rows = queries.shape[1]
    gqa = queries.shape[2] // (heads * HD)
    q_rows = STEPS * gqa * rows
    res_tok = res.shape[0]
    chunks = cfg["chunks"]
    nc = len(chunks)
    it = iter(scratch)
    pieces = sorted({chunk[:3] for chunk in chunks})
    pv = [next(it) for _ in pieces]
    s1 = [next(it) for _ in chunks]
    r1 = [next(it) for _ in chunks]
    s2 = [next(it) for _ in chunks]
    kcat, vcat, qcat, qv, fv, accs, sums, maxs, tab_v, tab_s = (next(it) for _ in range(10))
    rgroup_s, plen_v, rgroup_v, rlen = (next(it) for _ in range(4))
    load_sem, small_sem, send1, recv1, send2, recv2 = (next(it) for _ in range(6))

    seq, kvh, rep = lax.axis_index("seq"), lax.axis_index("kvh"), lax.axis_index("rep")
    zed, core = seq // CORES, lax.rem(seq, CORES)
    plane = [(a, b) for a in (2, 3, 1, 0) for b in (2, 1, 3, 0) if (a, b) != (0, 0)]
    line = [(a, b) for a in (4, 3, 5, 2, 6, 1, 7, 0) for b in (0, 1) if (a, b) != (0, 0)]

    kvh_peer = [kvh, kvh + 1 - 2 * lax.rem(kvh, 2), lax.rem(kvh + 2, 4), 3 - kvh]

    def plane_peer(off):
        return kvh_peer[off[0]], lax.rem(rep + off[1], n_rep)

    def first_slab(c):
        steps = chunks[c][3]
        return 0 if steps == ALL else 2 - 2 * (kvh // 2) if steps == (2, 3) else kvh_peer[steps[0]]

    def own_place(c):
        steps = chunks[c][3]
        return kvh if steps == ALL else lax.rem(kvh, 2) if steps == (2, 3) else 0

    def line_peer(off):
        return lax.rem(zed + off[0], n_z) * CORES + lax.rem(core + off[1], CORES)

    def loads(p):
        b, c0, w = pieces[p]
        return [
            pltpu.make_async_copy(
                prompt.at[:, pl.ds(b * BLK, BLK), pl.ds(k * width + c0, w)], pv[p].at[k], load_sem.at[p * n_kvh + k]
            )
            for k in range(n_kvh)
        ]

    small = [(groups_flat, rgroup_s), (groups_row, rgroup_v), (plen, plen_v), (res_len, rlen)]
    small = [pltpu.make_async_copy(a, b, small_sem.at[i]) for i, (a, b) in enumerate(small)]
    small[0].start()
    for copy in loads(0) + small[1:]:
        copy.start()
    others = []
    for h in range(heads):
        for at, dst in ((0, kcat), (HD, vcat)):
            others.append((res.at[:, pl.ds(2 * h * HD + at, HD)], dst.at[h, pl.ds(0, res_tok), pl.ds(0, HD)]))
    others += [(queries, qv), (fresh, fv)]
    others = [pltpu.make_async_copy(a, b, load_sem.at[len(pieces) * n_kvh + i]) for i, (a, b) in enumerate(others)]

    barrier = pltpu.get_barrier_semaphore()
    for off in plane:
        k2, r2 = plane_peer(off)
        pl.semaphore_signal(barrier, inc=1, device_id=(seq, k2, r2), device_id_type=MESH)
    for off in line:
        pl.semaphore_signal(barrier, inc=1, device_id=(line_peer(off), kvh, rep), device_id_type=MESH)

    small[0].wait()
    packed, power = [0] * n_rep, [1] * n_rep
    for q in range(n_req):
        to_rep = lax.rem(rgroup_s[rep * n_req + q], n_rep)
        for d in range(n_rep):
            hit = to_rep == lax.rem(rep + d, n_rep)
            packed[d] = packed[d] + jnp.where(hit, power[d] * q, 0)
            power[d] = jnp.where(hit, power[d] * n_req, power[d])
    bits = n_req.bit_length() - 1

    def request_at(d, j):
        return (packed[d] >> (bits * j)) & (n_req - 1)

    def send_plane(c):
        source, offs = pv[pieces.index(chunks[c][:3])], [off for off in plane if off[0] in chunks[c][3]]
        place = pl.ds((own_place(c) * n_rep + rep) * per_rep, per_rep)
        for i, off in enumerate(offs):
            k2, r2 = plane_peer(off)
            for j in range(per_rep):
                s1[c][i * per_rep + j] = source[k2, request_at(off[1], j)]
        if 0 in chunks[c][3]:
            for j in range(per_rep):
                r1[c][(own_place(c) * n_rep + rep) * per_rep + j] = source[kvh, request_at(0, j)]
        if c == 0:
            pl.semaphore_wait(barrier, len(plane) + len(line))
        for i, off in enumerate(offs):
            k2, r2 = plane_peer(off)
            pltpu.make_async_remote_copy(
                src_ref=s1[c].at[pl.ds(i * per_rep, per_rep)],
                dst_ref=r1[c].at[place],
                send_sem=send1.at[c],
                recv_sem=recv1.at[c],
                device_id=(seq, k2, r2),
                device_id_type=MESH,
            ).start()

    def landed_at(c, s, n, k):
        b, c0, w, steps = chunks[c]
        return land.at[pl.ds(s, n), pl.ds(k, len(steps)), pl.ds(b * BLK, BLK), pl.ds(c0, w)]

    def line_peers(c):
        if c < nc - LAST:
            return [line_peer(off) for off in line]
        peers = []
        for p in range(n_z - 1):
            z_to = nth_plane(p, zed)
            peers += [z_to * CORES + (p + 1) % 2, z_to * CORES + p % 2]
        return peers + [line_peer((0, 1))]

    def send_line(c):
        b, c0, w, steps = chunks[c]
        first = first_slab(c)
        peers = line_peers(c)
        for i, s_to in enumerate(peers + [seq]):
            slot, length = jnp.clip(tab_s[s_to, 0], 0, n_rep * per_rep - 1), tab_s[s_to, 1]
            for k in range(len(steps)):
                piece = r1[c][k * n_rep * per_rep + slot]
                at = (seq * n_kvh + first + k) * shard + b * BLK + iota((BLK, w), 0)
                piece = jnp.where(at < length, piece, jnp.zeros_like(piece))
                if i == len(peers):
                    land[seq, first + k, pl.ds(b * BLK, BLK), pl.ds(c0, w)] = piece
                else:
                    s2[c][i, k] = piece
        for i, s_to in enumerate(peers):
            pltpu.make_async_remote_copy(
                src_ref=s2[c].at[pl.ds(i, 1)],
                dst_ref=landed_at(c, seq, 1, first),
                send_sem=send2.at[c],
                recv_sem=recv2.at[c],
                device_id=(s_to, kvh, rep),
                device_id_type=MESH,
            ).start()

    loaded = set()

    def feed(c):
        if c < nc:
            p = pieces.index(chunks[c][:3])
            if p not in loaded:
                loaded.add(p)
                for copy in loads(p):
                    copy.wait()
            send_plane(c)

    for copy in small[1:]:
        copy.wait()
    total_req = rgroup_v.shape[1]
    groups = rgroup_v[...]
    mine = (lax.rem(groups, n_rep) == rep).astype(BF16)
    earlier = (iota((total_req, total_req), 0) < iota((total_req, total_req), 1)).astype(BF16)
    slots = jnp.dot(jnp.broadcast_to(mine, (n_seq, total_req)), earlier, preferred_element_type=F32)
    goes = jnp.broadcast_to(groups, (n_seq, total_req)) == iota((n_seq, total_req), 0) * n_rep + rep
    slot_of = jnp.sum(jnp.where(goes, slots, 0.0), axis=1, keepdims=True)
    len_of = jnp.sum(jnp.where(goes, plen_v[...].astype(F32), 0.0), axis=1, keepdims=True)
    lane = iota((n_seq, HD), 1)
    tab_v[...] = jnp.where(lane == 0, slot_of, len_of).astype(jnp.int32)
    to_smem = pltpu.make_async_copy(tab_v, tab_s, load_sem.at[len(pieces) * n_kvh + len(others)])
    to_smem.start()
    feed(0)
    for p in range(1, len(pieces)):
        for copy in loads(p):
            copy.start()
    for copy in others:
        copy.start()
    for c in range(1, cfg["ahead"]):
        feed(c)
    to_smem.wait()

    for c in range(nc):
        came = r1[c].at[pl.ds(0, s1[c].shape[0])]
        pltpu.make_async_copy(came, came, recv1.at[c]).wait()
        send_line(c)
        feed(c + cfg["ahead"])

    for copy in others:
        copy.wait()
    n_keys = kcat.shape[1]
    lens = rlen[...].astype(F32)
    diagonal = jnp.where(iota((rows, rows - 1), 0) == iota((rows, rows - 1), 1), lens, 0.0)
    column = jnp.sum(diagonal, axis=1, keepdims=True)
    above = iota((rows, HD), 0) - iota((rows, HD), 1)
    ends = jnp.sum(jnp.where(above <= 0, column, 0.0), axis=0, keepdims=True).astype(jnp.int32)
    starts = jnp.sum(jnp.where(above < 0, column, 0.0), axis=0, keepdims=True).astype(jnp.int32)

    def hide(i, carry):
        key = i * 256 + iota((256, HD), 0)
        hidden = ((key < starts) | (key >= ends)) & (iota((256, HD), 1) < rows)
        hidden = hidden.astype(F32).astype(BF16)
        at = pl.ds(pl.multiple_of(i * 256, 256), 256)
        for h in range(heads):
            kcat[h, at, pl.ds(HD, HD)] = hidden
            vcat[h, at, pl.ds(HD, HD)] = jnp.ones((256, HD), BF16)
        return carry

    lax.fori_loop(0, res_tok // 256, hide, 0)
    rest = n_keys - res_tok
    key, lane = iota((rest, HD), 0), iota((rest, HD), 1)
    hidden = ((lane < rows) & (lane != lax.rem(key, rows))) | ((lane == rows) & (key >= rows)) | (
        (lane == rows + 1) & (key >= STEPS * rows)
    )
    hidden = hidden.astype(F32).astype(BF16)
    pad = jnp.zeros((rest - STEPS * rows, HD), BF16)
    for h in range(heads):
        kcat[h, pl.ds(res_tok, rest), pl.ds(HD, HD)] = hidden
        vcat[h, pl.ds(res_tok, rest), pl.ds(HD, HD)] = jnp.ones((rest, HD), BF16)
        for at, dst in ((0, kcat), (HD, vcat)):
            for u in range(STEPS):
                dst[h, pl.ds(res_tok + u * rows, rows), pl.ds(0, HD)] = fv[u, :, pl.ds(2 * h * HD + at, HD)]
            dst[h, pl.ds(res_tok + STEPS * rows, rest - STEPS * rows), pl.ds(0, HD)] = pad
    row, lane = iota((rows, HD), 0), iota((rows, HD), 1)
    for t in range(STEPS):
        aside = (lane == row) | (lane == rows + 1)
        if t == 0:
            aside = aside | (lane == rows)
        aside = jnp.where(aside, NEG, 0.0).astype(BF16)
        for h in range(heads):
            for g in range(gqa):
                at = pl.ds((t * gqa + g) * rows, rows)
                qcat[h, at, pl.ds(0, HD)] = qv[t, :, pl.ds((h * gqa + g) * HD, HD)]
                qcat[h, at, pl.ds(HD, HD)] = aside

    q_tile = cfg["q_tile"]
    tiles = q_rows // q_tile

    def attend(i, carry):
        h, at = i // tiles, pl.ds(pl.multiple_of(lax.rem(i, tiles) * q_tile, q_tile), q_tile)
        scores = lax.dot_general(qcat[h, at, :], kcat[h], NT, preferred_element_type=F32)
        top = jnp.max(scores, axis=1, keepdims=True)
        weights = jnp.exp2((scores - top) * EXP2_SCALE).astype(BF16)
        mixed = jnp.dot(weights, vcat[h], preferred_element_type=F32)
        accs[h, at, :] = mixed[:, :HD]
        sums[h, at, :] = mixed[:, HD:]
        maxs[h, at, :] = jnp.broadcast_to(top, (q_tile, HD))
        return carry

    lax.fori_loop(0, heads * tiles, attend, 0)

    few = STEPS * gqa
    pick = (iota((few, q_rows), 1) == iota((few, q_rows), 0) * rows + (rows - 1)).astype(F32).astype(BF16)
    last = pl.ds(rows - 1, few, stride=rows)
    own_len = tab_s[seq, 1]
    asks, parts = [], []
    for h in range(heads):
        asks.append(jnp.dot(pick, qcat[h, :, pl.ds(0, HD)], preferred_element_type=F32).astype(BF16))
        parts.append([(maxs[h, last, :], sums[h, last, :], accs[h, last, :])])
    for h in range(heads):
        accs[h] = accs[h] / sums[h]

    keys_blk = n_seq * n_kvh * BLK
    n_at = iota((few, keys_blk), 1)
    n_at = (n_at // BLK) * shard + lax.rem(n_at, BLK)
    arrived = set()
    for c, (b, c0, w, steps) in enumerate(chunks):
        came = landed_at(c, 0, len(line), 0)
        pltpu.make_async_copy(came, came, recv2.at[c]).wait()
        if steps in (ALL, (2, 3)):
            arrived |= {(b, at) for at in range(c0, c0 + w, HD)}
        for h in range(heads):
            k_at, v_at = 2 * h * HD, (2 * h + 1) * HD
            if not {(b, k_at), (b, v_at)} <= arrived:
                continue
            arrived -= {(b, k_at), (b, v_at)}
            keys = land[:, :, pl.ds(b * BLK, BLK), pl.ds(k_at, HD)].reshape(keys_blk, HD)
            values = land[:, :, pl.ds(b * BLK, BLK), pl.ds(v_at, HD)].reshape(keys_blk, HD)
            scores = lax.dot_general(asks[h], keys, NT, preferred_element_type=F32)
            scores = jnp.where(n_at + b * BLK < own_len, scores, NEG)
            top = jnp.max(scores, axis=1, keepdims=True)
            weights = jnp.exp2((scores - top) * EXP2_SCALE)
            total = jnp.sum(weights, axis=1, keepdims=True)
            mixed = jnp.dot(weights.astype(BF16), values, preferred_element_type=F32)
            parts[h].append((top, total, mixed))
    for h in range(heads):
        top = functools.reduce(jnp.maximum, [m for m, _, _ in parts[h]])
        total, mixed = 0.0, 0.0
        for m, l, a in parts[h]:
            factor = jnp.exp2((m - top) * EXP2_SCALE)
            total, mixed = total + factor * l, mixed + factor * a
        accs[h, last, :] = mixed / total
        for t in range(STEPS):
            for g in range(gqa):
                attv[t, :, pl.ds((h * gqa + g) * HD, HD)] = accs[h, pl.ds((t * gqa + g) * rows, rows), :].astype(BF16)
    for c in range(nc):
        pltpu.make_async_copy(s1[c], s1[c], send1.at[c]).wait()
        pltpu.make_async_copy(s2[c], s2[c], send2.at[c]).wait()


def store(attv, land, att_out, land_out, sem):
    copies = [pltpu.make_async_copy(attv, att_out, sem.at[0])]
    parts = land.shape[0] // 4
    for i in range(parts):
        copies.append(pltpu.make_async_copy(land.at[pl.ds(i * 4, 4)], land_out.at[pl.ds(i * 4, 4)], sem.at[1 + i]))
    for copy in copies:
        copy.start()
    for copy in copies:
        copy.wait()


def per_device(mesh_shape, prompt_kv, prompt_len, request_group, res_kv, res_len, queries, step_kv):
    n_seq, n_kvh, n_rep = mesh_shape
    n_req, shard, all_cols = prompt_kv.shape
    width = all_cols // n_kvh
    per_rep = n_req // n_rep
    heads = width // (2 * HD)
    blocks = shard // BLK
    rows, q_cols = queries.shape[1:]
    q_rows = STEPS * rows * (q_cols // (heads * HD))
    chunks = CHUNKS
    n_keys = res_kv.shape[0] + 256
    cfg = dict(mesh=mesh_shape, chunks=chunks, q_tile=128, ahead=AHEAD)
    pieces = sorted({chunk[:3] for chunk in chunks})
    v = lambda shape, dtype=BF16: pltpu.VMEM(shape, dtype)
    dma = lambda n: pltpu.SemaphoreType.DMA((n,))
    scratch = (
        [v((n_kvh, n_req, BLK, w)) for _, _, w in pieces]
        + [v(((len(d) * n_rep - (0 in d)) * per_rep, BLK, w)) for _, _, w, d in chunks]
        + [v((len(d) * n_rep * per_rep, BLK, w)) for _, _, w, d in chunks]
        + [v((n_seq - 1, len(d), BLK, w)) for _, _, w, d in chunks]
        + [
            v((heads, n_keys, 2 * HD)),
            v((heads, n_keys, 2 * HD)),
            v((heads, q_rows, 2 * HD)),
            v(queries.shape),
            v(step_kv.shape),
            v((heads, q_rows, HD), F32),
            v((heads, q_rows, HD), F32),
            v((heads, q_rows, HD), F32),
            v((n_seq, HD), jnp.int32),
            pltpu.SMEM((n_seq, HD), jnp.int32),
            pltpu.SMEM(request_group.shape, jnp.int32),
            v((1, request_group.shape[0]), jnp.int32),
            v((1, request_group.shape[0]), jnp.int32),
            v(res_len.shape, jnp.int32),
        ]
        + [dma(len(pieces) * n_kvh + 2 * heads + 3), dma(4)]
        + [dma(len(chunks))] * 4
    )
    spec = lambda space: pl.BlockSpec(memory_space=space)
    held = pl.pallas_call(
        functools.partial(kernel, cfg),
        out_shape=(
            pltpu.VMEM(queries.shape, BF16),
            pltpu.VMEM((n_seq, n_kvh, shard, width), BF16),
        ),
        in_specs=[spec(pl.ANY)] * 8,
        out_specs=(spec(pltpu.VMEM), spec(pltpu.VMEM)),
        scratch_shapes=scratch,
        compiler_params=pltpu.CompilerParams(collective_id=0, has_side_effects=True, vmem_limit_bytes=58 << 20),
    )(
        prompt_kv,
        request_group,
        prompt_len.reshape(1, -1),
        request_group.reshape(1, -1),
        res_kv,
        res_len,
        queries,
        step_kv,
    )
    attention, landed = pl.pallas_call(
        store,
        out_shape=tuple(jax.ShapeDtypeStruct(a.shape, a.dtype) for a in held),
        in_specs=[spec(pltpu.VMEM)] * 2,
        out_specs=(spec(pl.ANY), spec(pl.ANY)),
        scratch_shapes=[dma(1 + n_seq // 4)],
        compiler_params=pltpu.CompilerParams(vmem_limit_bytes=2 << 20),
    )(*held)
    return attention, landed.reshape(n_seq * n_kvh * shard, width)


def solution(mesh):
    in_specs = (
        P("rep", ("seq", "kvh"), None),
        P(),
        P(),
        P(("seq", "rep"), "kvh"),
        P(("seq", "rep"), None),
        P(None, ("seq", "rep"), "kvh"),
        P(None, ("seq", "rep"), "kvh"),
    )
    out_specs = (P(None, ("seq", "rep"), "kvh"), P(("seq", "rep"), "kvh"))
    shape = tuple(mesh.shape[a] for a in ("seq", "kvh", "rep"))
    return jax.shard_map(
        functools.partial(per_device, shape), mesh=mesh, in_specs=in_specs, out_specs=out_specs, check_vma=False
    )
```

```python
import functools
import jax
import jax.numpy as jnp
from jax import lax
from jax.experimental import pallas as pl
from jax.experimental.pallas import tpu as pltpu
from jax.sharding import PartitionSpec as P

HD = 128
STEPS = 2
CORES = 2
BLK = 16
NEG = -1e30
MESH = pl.DeviceIdType.MESH
EXP2_SCALE = (HD ** -0.5) * 1.4426950408889634
BF16 = jnp.bfloat16
F32 = jnp.float32
NT = (((1,), (1,)), ((), ()))
AHEAD = 4
LAST = 2
LATE_ORDER = [0, 1, 2, 3, 4, 5, 6, 7]
ALL = (0, 1, 2, 3)
CHUNKS = [
    (0, 0, 128, (0,)),
    (0, 0, 128, (1,)),
    (0, 0, 128, (2, 3)),
    (0, 128, 128, ALL),
    (0, 256, 256, ALL),
    (1, 0, 512, ALL),
    (2, 0, 256, ALL),
    (2, 256, 256, ALL),
]


def packed(values):
    return sum(v << (3 * i) for i, v in enumerate(values))


def nth_plane(p, zed):
    own = (packed([LATE_ORDER.index(i) for i in range(8)]) >> (3 * zed)) & 7
    at = p + (p >= own).astype(jnp.int32)
    return (packed(LATE_ORDER) >> (3 * at)) & 7


def wrap(value, size):
    return lax.rem(value + size, size)


def iota(shape, dim):
    return lax.broadcasted_iota(jnp.int32, shape, dim)


def kernel(cfg, prompt, groups_flat, plen, groups_row, res, res_len, queries, fresh, attv, land, *scratch):
    n_seq, n_kvh, n_rep = cfg["mesh"]
    n_z = n_seq // CORES
    n_req, shard, _ = prompt.shape
    width = land.shape[3]
    blocks = shard // BLK
    per_rep = n_req // n_rep
    heads = width // (2 * HD)
    rows = queries.shape[1]
    gqa = queries.shape[2] // (heads * HD)
    q_rows = STEPS * gqa * rows
    res_tok = res.shape[0]
    chunks = cfg["chunks"]
    nc = len(chunks)
    it = iter(scratch)
    pieces = sorted({chunk[:3] for chunk in chunks})
    pv = [next(it) for _ in pieces]
    s1 = [next(it) for _ in chunks]
    r1 = [next(it) for _ in chunks]
    s2 = [next(it) for _ in chunks]
    kcat, vcat, qcat, qv, fv, accs, sums, maxs, tab_v, tab_s = (next(it) for _ in range(10))
    rgroup_s, plen_v, rgroup_v, rlen = (next(it) for _ in range(4))
    load_sem, small_sem, send1, recv1, send2, recv2 = (next(it) for _ in range(6))

    seq, kvh, rep = lax.axis_index("seq"), lax.axis_index("kvh"), lax.axis_index("rep")
    zed, core = seq // CORES, lax.rem(seq, CORES)
    plane = [(a, b) for a in (2, 3, 1, 0) for b in (2, 1, 3, 0) if (a, b) != (0, 0)]
    line = [(a, b) for a in (4, 3, 5, 2, 6, 1, 7, 0) for b in (0, 1) if (a, b) != (0, 0)]

    kvh_peer = [kvh, kvh + 1 - 2 * lax.rem(kvh, 2), lax.rem(kvh + 2, 4), 3 - kvh]

    def plane_peer(off):
        return kvh_peer[off[0]], lax.rem(rep + off[1], n_rep)

    def first_slab(c):
        steps = chunks[c][3]
        return 0 if steps == ALL else 2 - 2 * (kvh // 2) if steps == (2, 3) else kvh_peer[steps[0]]

    def own_place(c):
        steps = chunks[c][3]
        return kvh if steps == ALL else lax.rem(kvh, 2) if steps == (2, 3) else 0

    def line_peer(off):
        return lax.rem(zed + off[0], n_z) * CORES + lax.rem(core + off[1], CORES)

    def loads(p):
        b, c0, w = pieces[p]
        return [
            pltpu.make_async_copy(
                prompt.at[:, pl.ds(b * BLK, BLK), pl.ds(k * width + c0, w)], pv[p].at[k], load_sem.at[p * n_kvh + k]
            )
            for k in range(n_kvh)
        ]

    small = [(groups_flat, rgroup_s), (groups_row, rgroup_v), (plen, plen_v), (res_len, rlen)]
    small = [pltpu.make_async_copy(a, b, small_sem.at[i]) for i, (a, b) in enumerate(small)]
    small[0].start()
    for copy in loads(0) + small[1:]:
        copy.start()
    others = []
    for h in range(heads):
        for at, dst in ((0, kcat), (HD, vcat)):
            others.append((res.at[:, pl.ds(2 * h * HD + at, HD)], dst.at[h, pl.ds(0, res_tok), pl.ds(0, HD)]))
    others += [(queries, qv), (fresh, fv)]
    others = [pltpu.make_async_copy(a, b, load_sem.at[len(pieces) * n_kvh + i]) for i, (a, b) in enumerate(others)]

    barrier = pltpu.get_barrier_semaphore()
    for off in plane:
        k2, r2 = plane_peer(off)
        pl.semaphore_signal(barrier, inc=1, device_id=(seq, k2, r2), device_id_type=MESH)
    for off in line:
        pl.semaphore_signal(barrier, inc=1, device_id=(line_peer(off), kvh, rep), device_id_type=MESH)

    small[0].wait()
    packed, power = [0] * n_rep, [1] * n_rep
    for q in range(n_req):
        to_rep = lax.rem(rgroup_s[rep * n_req + q], n_rep)
        for d in range(n_rep):
            hit = to_rep == lax.rem(rep + d, n_rep)
            packed[d] = packed[d] + jnp.where(hit, power[d] * q, 0)
            power[d] = jnp.where(hit, power[d] * n_req, power[d])
    bits = n_req.bit_length() - 1

    def request_at(d, j):
        return (packed[d] >> (bits * j)) & (n_req - 1)

    def send_plane(c):
        source, offs = pv[pieces.index(chunks[c][:3])], [off for off in plane if off[0] in chunks[c][3]]
        place = pl.ds((own_place(c) * n_rep + rep) * per_rep, per_rep)
        for i, off in enumerate(offs):
            k2, r2 = plane_peer(off)
            for j in range(per_rep):
                s1[c][i * per_rep + j] = source[k2, request_at(off[1], j)]
        if 0 in chunks[c][3]:
            for j in range(per_rep):
                r1[c][(own_place(c) * n_rep + rep) * per_rep + j] = source[kvh, request_at(0, j)]
        if c == 0:
            pl.semaphore_wait(barrier, len(plane) + len(line))
        for i, off in enumerate(offs):
            k2, r2 = plane_peer(off)
            pltpu.make_async_remote_copy(
                src_ref=s1[c].at[pl.ds(i * per_rep, per_rep)],
                dst_ref=r1[c].at[place],
                send_sem=send1.at[c],
                recv_sem=recv1.at[c],
                device_id=(seq, k2, r2),
                device_id_type=MESH,
            ).start()

    def landed_at(c, s, n, k):
        b, c0, w, steps = chunks[c]
        return land.at[pl.ds(s, n), pl.ds(k, len(steps)), pl.ds(b * BLK, BLK), pl.ds(c0, w)]

    def line_peers(c):
        if c < nc - LAST:
            steps = [a + core * (b - a) for a, b in zip((4, 3, 2, 1, 5, 6, 7), (4, 5, 6, 7, 3, 2, 1))]
            return [line_peer((a, b)) for a in steps for b in (0, 1)] + [line_peer((0, 1))]
        peers = []
        for p, half in ((0, 1), (0, 0), (1, 1), (2, 1), (1, 0), (2, 0), (3, 0), (3, 1), (4, 0), (4, 1), (5, 0), (5, 1), (6, 0), (6, 1)):
            peers.append(nth_plane(p, zed) * CORES + half)
        return peers + [line_peer((0, 1))]

    def send_line(c):
        b, c0, w, steps = chunks[c]
        first = first_slab(c)
        peers = line_peers(c)
        for i, s_to in enumerate(peers + [seq]):
            slot, length = jnp.clip(tab_s[s_to, 0], 0, n_rep * per_rep - 1), tab_s[s_to, 1]
            for k in range(len(steps)):
                piece = r1[c][k * n_rep * per_rep + slot]
                at = (seq * n_kvh + first + k) * shard + b * BLK + iota((BLK, w), 0)
                piece = jnp.where(at < length, piece, jnp.zeros_like(piece))
                if i == len(peers):
                    land[seq, first + k, pl.ds(b * BLK, BLK), pl.ds(c0, w)] = piece
                else:
                    s2[c][i, k] = piece
        for i, s_to in enumerate(peers):
            pltpu.make_async_remote_copy(
                src_ref=s2[c].at[pl.ds(i, 1)],
                dst_ref=landed_at(c, seq, 1, first),
                send_sem=send2.at[c],
                recv_sem=recv2.at[c],
                device_id=(s_to, kvh, rep),
                device_id_type=MESH,
            ).start()

    loaded = set()

    def feed(c):
        if c < nc:
            p = pieces.index(chunks[c][:3])
            if p not in loaded:
                loaded.add(p)
                for copy in loads(p):
                    copy.wait()
            send_plane(c)

    feed(0)
    for p in range(1, len(pieces)):
        for copy in loads(p):
            copy.start()

    for copy in small[1:]:
        copy.wait()
    total_req = rgroup_v.shape[1]
    groups = rgroup_v[...]
    mine = (lax.rem(groups, n_rep) == rep).astype(BF16)
    earlier = (iota((total_req, total_req), 0) < iota((total_req, total_req), 1)).astype(BF16)
    slots = jnp.dot(jnp.broadcast_to(mine, (n_seq, total_req)), earlier, preferred_element_type=F32)
    goes = jnp.broadcast_to(groups, (n_seq, total_req)) == iota((n_seq, total_req), 0) * n_rep + rep
    slot_of = jnp.sum(jnp.where(goes, slots, 0.0), axis=1, keepdims=True)
    len_of = jnp.sum(jnp.where(goes, plen_v[...].astype(F32), 0.0), axis=1, keepdims=True)
    lane = iota((n_seq, HD), 1)
    tab_v[...] = jnp.where(lane == 0, slot_of, len_of).astype(jnp.int32)
    to_smem = pltpu.make_async_copy(tab_v, tab_s, load_sem.at[len(pieces) * n_kvh + len(others)])
    to_smem.start()
    for c in range(1, cfg["ahead"]):
        feed(c)
    to_smem.wait()

    for c in range(nc):
        came = r1[c].at[pl.ds(0, s1[c].shape[0])]
        pltpu.make_async_copy(came, came, recv1.at[c]).wait()
        send_line(c)
        if c == 0:
            for copy in others:
                copy.start()
        feed(c + cfg["ahead"])

    for copy in others:
        copy.wait()
    n_keys = kcat.shape[1]
    lens = rlen[...].astype(F32)
    diagonal = jnp.where(iota((rows, rows - 1), 0) == iota((rows, rows - 1), 1), lens, 0.0)
    column = jnp.sum(diagonal, axis=1, keepdims=True)
    above = iota((rows, HD), 0) - iota((rows, HD), 1)
    ends = jnp.sum(jnp.where(above <= 0, column, 0.0), axis=0, keepdims=True).astype(jnp.int32)
    starts = jnp.sum(jnp.where(above < 0, column, 0.0), axis=0, keepdims=True).astype(jnp.int32)

    def hide(i, carry):
        key = i * 256 + iota((256, HD), 0)
        hidden = ((key < starts) | (key >= ends)) & (iota((256, HD), 1) < rows)
        hidden = hidden.astype(F32).astype(BF16)
        at = pl.ds(pl.multiple_of(i * 256, 256), 256)
        for h in range(heads):
            kcat[h, at, pl.ds(HD, HD)] = hidden
            vcat[h, at, pl.ds(HD, HD)] = jnp.ones((256, HD), BF16)
        return carry

    lax.fori_loop(0, res_tok // 256, hide, 0)
    rest = n_keys - res_tok
    key, lane = iota((rest, HD), 0), iota((rest, HD), 1)
    hidden = ((lane < rows) & (lane != lax.rem(key, rows))) | ((lane == rows) & (key >= rows)) | (
        (lane == rows + 1) & (key >= STEPS * rows)
    )
    hidden = hidden.astype(F32).astype(BF16)
    pad = jnp.zeros((rest - STEPS * rows, HD), BF16)
    for h in range(heads):
        kcat[h, pl.ds(res_tok, rest), pl.ds(HD, HD)] = hidden
        vcat[h, pl.ds(res_tok, rest), pl.ds(HD, HD)] = jnp.ones((rest, HD), BF16)
        for at, dst in ((0, kcat), (HD, vcat)):
            for u in range(STEPS):
                dst[h, pl.ds(res_tok + u * rows, rows), pl.ds(0, HD)] = fv[u, :, pl.ds(2 * h * HD + at, HD)]
            dst[h, pl.ds(res_tok + STEPS * rows, rest - STEPS * rows), pl.ds(0, HD)] = pad
    row, lane = iota((rows, HD), 0), iota((rows, HD), 1)
    for t in range(STEPS):
        aside = (lane == row) | (lane == rows + 1)
        if t == 0:
            aside = aside | (lane == rows)
        aside = jnp.where(aside, NEG, 0.0).astype(BF16)
        for h in range(heads):
            for g in range(gqa):
                at = pl.ds((t * gqa + g) * rows, rows)
                qcat[h, at, pl.ds(0, HD)] = qv[t, :, pl.ds((h * gqa + g) * HD, HD)]
                qcat[h, at, pl.ds(HD, HD)] = aside

    q_tile = cfg["q_tile"]
    tiles = q_rows // q_tile

    def attend(i, carry):
        h, at = i // tiles, pl.ds(pl.multiple_of(lax.rem(i, tiles) * q_tile, q_tile), q_tile)
        scores = lax.dot_general(qcat[h, at, :], kcat[h], NT, preferred_element_type=F32)
        top = jnp.max(scores, axis=1, keepdims=True)
        weights = jnp.exp2((scores - top) * EXP2_SCALE).astype(BF16)
        mixed = jnp.dot(weights, vcat[h], preferred_element_type=F32)
        accs[h, at, :] = mixed[:, :HD]
        sums[h, at, :] = mixed[:, HD:]
        maxs[h, at, :] = jnp.broadcast_to(top, (q_tile, HD))
        return carry

    lax.fori_loop(0, heads * tiles, attend, 0)

    few = STEPS * gqa
    pick = (iota((few, q_rows), 1) == iota((few, q_rows), 0) * rows + (rows - 1)).astype(F32).astype(BF16)
    last = pl.ds(rows - 1, few, stride=rows)
    own_len = tab_s[seq, 1]
    asks, parts = [], []
    for h in range(heads):
        asks.append(jnp.dot(pick, qcat[h, :, pl.ds(0, HD)], preferred_element_type=F32).astype(BF16))
        parts.append([(maxs[h, last, :], sums[h, last, :], accs[h, last, :])])
    for h in range(heads):
        accs[h] = accs[h] / sums[h]

    keys_blk = n_seq * n_kvh * BLK
    n_at = iota((few, keys_blk), 1)
    n_at = (n_at // BLK) * shard + lax.rem(n_at, BLK)
    arrived = set()
    for c, (b, c0, w, steps) in enumerate(chunks):
        came = landed_at(c, 0, len(line), 0)
        pltpu.make_async_copy(came, came, recv2.at[c]).wait()
        if steps in (ALL, (2, 3)):
            arrived |= {(b, at) for at in range(c0, c0 + w, HD)}
        for h in range(heads):
            k_at, v_at = 2 * h * HD, (2 * h + 1) * HD
            if not {(b, k_at), (b, v_at)} <= arrived:
                continue
            arrived -= {(b, k_at), (b, v_at)}
            keys = land[:, :, pl.ds(b * BLK, BLK), pl.ds(k_at, HD)].reshape(keys_blk, HD)
            values = land[:, :, pl.ds(b * BLK, BLK), pl.ds(v_at, HD)].reshape(keys_blk, HD)
            scores = lax.dot_general(asks[h], keys, NT, preferred_element_type=F32)
            scores = jnp.where(n_at + b * BLK < own_len, scores, NEG)
            top = jnp.max(scores, axis=1, keepdims=True)
            weights = jnp.exp2((scores - top) * EXP2_SCALE)
            total = jnp.sum(weights, axis=1, keepdims=True)
            mixed = jnp.dot(weights.astype(BF16), values, preferred_element_type=F32)
            parts[h].append((top, total, mixed))
    for h in range(heads):
        top = functools.reduce(jnp.maximum, [m for m, _, _ in parts[h]])
        total, mixed = 0.0, 0.0
        for m, l, a in parts[h]:
            factor = jnp.exp2((m - top) * EXP2_SCALE)
            total, mixed = total + factor * l, mixed + factor * a
        accs[h, last, :] = mixed / total
        for t in range(STEPS):
            for g in range(gqa):
                attv[t, :, pl.ds((h * gqa + g) * HD, HD)] = accs[h, pl.ds((t * gqa + g) * rows, rows), :].astype(BF16)
    for c in range(nc):
        pltpu.make_async_copy(s1[c], s1[c], send1.at[c]).wait()
        pltpu.make_async_copy(s2[c], s2[c], send2.at[c]).wait()


def store(attv, land, att_out, land_out, sem):
    copies = [pltpu.make_async_copy(attv, att_out, sem.at[0])]
    parts = land.shape[0] // 4
    for i in range(parts):
        copies.append(pltpu.make_async_copy(land.at[pl.ds(i * 4, 4)], land_out.at[pl.ds(i * 4, 4)], sem.at[1 + i]))
    for copy in copies:
        copy.start()
    for copy in copies:
        copy.wait()


def per_device(mesh_shape, prompt_kv, prompt_len, request_group, res_kv, res_len, queries, step_kv):
    n_seq, n_kvh, n_rep = mesh_shape
    n_req, shard, all_cols = prompt_kv.shape
    width = all_cols // n_kvh
    per_rep = n_req // n_rep
    heads = width // (2 * HD)
    blocks = shard // BLK
    rows, q_cols = queries.shape[1:]
    q_rows = STEPS * rows * (q_cols // (heads * HD))
    chunks = CHUNKS
    n_keys = res_kv.shape[0] + 256
    cfg = dict(mesh=mesh_shape, chunks=chunks, q_tile=128, ahead=AHEAD)
    pieces = sorted({chunk[:3] for chunk in chunks})
    v = lambda shape, dtype=BF16: pltpu.VMEM(shape, dtype)
    dma = lambda n: pltpu.SemaphoreType.DMA((n,))
    scratch = (
        [v((n_kvh, n_req, BLK, w)) for _, _, w in pieces]
        + [v(((len(d) * n_rep - (0 in d)) * per_rep, BLK, w)) for _, _, w, d in chunks]
        + [v((len(d) * n_rep * per_rep, BLK, w)) for _, _, w, d in chunks]
        + [v((n_seq - 1, len(d), BLK, w)) for _, _, w, d in chunks]
        + [
            v((heads, n_keys, 2 * HD)),
            v((heads, n_keys, 2 * HD)),
            v((heads, q_rows, 2 * HD)),
            v(queries.shape),
            v(step_kv.shape),
            v((heads, q_rows, HD), F32),
            v((heads, q_rows, HD), F32),
            v((heads, q_rows, HD), F32),
            v((n_seq, HD), jnp.int32),
            pltpu.SMEM((n_seq, HD), jnp.int32),
            pltpu.SMEM(request_group.shape, jnp.int32),
            v((1, request_group.shape[0]), jnp.int32),
            v((1, request_group.shape[0]), jnp.int32),
            v(res_len.shape, jnp.int32),
        ]
        + [dma(len(pieces) * n_kvh + 2 * heads + 3), dma(4)]
        + [dma(len(chunks))] * 4
    )
    spec = lambda space: pl.BlockSpec(memory_space=space)
    held = pl.pallas_call(
        functools.partial(kernel, cfg),
        out_shape=(
            pltpu.VMEM(queries.shape, BF16),
            pltpu.VMEM((n_seq, n_kvh, shard, width), BF16),
        ),
        in_specs=[spec(pl.ANY)] * 8,
        out_specs=(spec(pltpu.VMEM), spec(pltpu.VMEM)),
        scratch_shapes=scratch,
        compiler_params=pltpu.CompilerParams(collective_id=0, has_side_effects=True, vmem_limit_bytes=58 << 20),
    )(
        prompt_kv,
        request_group,
        prompt_len.reshape(1, -1),
        request_group.reshape(1, -1),
        res_kv,
        res_len,
        queries,
        step_kv,
    )
    attention, landed = pl.pallas_call(
        store,
        out_shape=tuple(jax.ShapeDtypeStruct(a.shape, a.dtype) for a in held),
        in_specs=[spec(pltpu.VMEM)] * 2,
        out_specs=(spec(pl.ANY), spec(pl.ANY)),
        scratch_shapes=[dma(1 + n_seq // 4)],
        compiler_params=pltpu.CompilerParams(vmem_limit_bytes=2 << 20),
    )(*held)
    return attention, landed.reshape(n_seq * n_kvh * shard, width)


def solution(mesh):
    in_specs = (
        P("rep", ("seq", "kvh"), None),
        P(),
        P(),
        P(("seq", "rep"), "kvh"),
        P(("seq", "rep"), None),
        P(None, ("seq", "rep"), "kvh"),
        P(None, ("seq", "rep"), "kvh"),
    )
    out_specs = (P(None, ("seq", "rep"), "kvh"), P(("seq", "rep"), "kvh"))
    shape = tuple(mesh.shape[a] for a in ("seq", "kvh", "rep"))
    return jax.shard_map(
        functools.partial(per_device, shape), mesh=mesh, in_specs=in_specs, out_specs=out_specs, check_vma=False
    )
```
